128 devices in a mesh: out: 8 (over x, z_lo), in: 16 (over y, z_hi, core).
Axes of the slice: x: 4, y: 4, z: 4 (z_hi: 2, z_lo: 2; z = z_hi * 2 + z_lo), core: 2. Of those that a mesh axis runs over, the one named last changes fastest.
Arguments:
- out_grads: bfloat16 [1024, 28672], P('out', 'in'), may hold values from -2 to 2
- layer_inputs: bfloat16 [1024, 8192], P('in', 'out'), may hold values from -2 to 2
- basis_out: bfloat16 [28672, 28672], P('in', 'out'), may hold values from -0.03125 to 0.03125
- basis_in: bfloat16 [8192, 8192], P('out', 'in'), may hold values from -0.0625 to 0.0625
Outputs:
- eigen_correction: float32 [28672, 8192], P('out', 'in')
The draws below stay inside these ranges and needn't reach their ends.
All inputs are finite; a program needn't handle non-finite values.
Results may differ from the reference program's by a relative error of at most 0.0029.
Values may be sent and summed in bfloat16 or wider, within the bound.
No kernel may reach another device: no remote copies, remote signals or barrier semaphores. Data moves between devices by JAX's collectives and lax.ppermute only.
A program may use at most 128 MiB of HBM per device.

```python
import jax
import jax.numpy as jnp
from jax import lax

OUT = 28672
IN = 8192
SEQ_LEN = 128
SEQS = 8
TOKENS = 1024


def steps_of(stream_key, shape, cuts, smallest, largest):
    def one(dim, shards_of):
        draws = jax.random.uniform(jax.random.fold_in(jax.random.fold_in(stream_key, 6), dim), (shards_of,), jnp.float32, smallest / len(cuts), largest / len(cuts))
        return jnp.repeat(jnp.exp(draws), shape[dim] // shards_of).reshape((-1,) + (1,) * (len(shape) - dim - 1))

    level = one(*cuts[0])
    for cut in cuts[1:]:
        level = level * one(*cut)
    return level


def gaussian(own_key, dims, width, bound, cuts=(), held_as=jnp.bfloat16):
    result = jax.random.normal(own_key, dims, jnp.float32) * width
    if len(cuts) > 0:
        result = steps_of(own_key, dims, cuts, -0.22, 0.18) * result
    return jnp.clip(result, min=-bound, max=bound).astype(held_as)


def setup_inputs(seed: int = 0) -> dict:
    arg_keys = jax.random.split(jax.random.key(seed), 5)
    return {
        "out_grads": gaussian(arg_keys[0], (TOKENS, OUT), 0.3, 2.0, ((0, 8), (1, 16))),
        "layer_inputs": gaussian(arg_keys[1], (TOKENS, IN), 0.3, 2.0, ((0, 16), (1, 8))),
        "basis_out": gaussian(arg_keys[2], (OUT, OUT), OUT ** -0.5, 0.03125, ((0, 16), (1, 8))),
        "basis_in": gaussian(arg_keys[3], (IN, IN), IN ** -0.5, 0.0625, ((0, 8), (1, 16))),
    }


def reference(out_grads, layer_inputs, basis_out, basis_in):
    block = OUT // 8
    grads_wide = out_grads.astype(jnp.float32)

    def rotate_block(index):
        columns = lax.dynamic_slice_in_dim(basis_out, (index * block).astype(jnp.int32), block, 1)
        return jnp.dot(grads_wide, columns.astype(jnp.float32)).astype(jnp.bfloat16)

    pieces = lax.map(rotate_block, jnp.arange(8, dtype=jnp.int32))
    rotated_grads = jnp.concatenate([pieces[i] for i in range(8)], axis=1)
    rotated_inputs = jnp.dot(layer_inputs.astype(jnp.float32), basis_in.astype(jnp.float32)).astype(jnp.bfloat16)

    def add_sequence(index, total):
        first = (index * SEQ_LEN).astype(jnp.int32)
        grad_rows = lax.dynamic_slice_in_dim(rotated_grads, first, SEQ_LEN, 0).astype(jnp.float32)
        input_rows = lax.dynamic_slice_in_dim(rotated_inputs, first, SEQ_LEN, 0).astype(jnp.float32)
        product = jnp.dot(grad_rows.T, input_rows)
        return total + product * product

    total = lax.fori_loop(0, SEQS, add_sequence, jnp.zeros((OUT, IN), jnp.float32))
    return total / jnp.float32(SEQS)
```

```python
import jax
import jax.numpy as jnp
from jax import lax
from jax.experimental import pallas as pl
from jax.experimental.pallas import tpu as pltpu
from jax.sharding import Mesh
from jax.sharding import PartitionSpec as P

SEQ_LEN = 128
NX, NZL, NY, NZH, NC = 4, 2, 4, 2, 2
BLK = SEQ_LEN // (NY * NC)
BF = jnp.bfloat16
F32 = jnp.float32


def swap(v, axis):
    return lax.ppermute(v, axis, [(0, 1), (1, 0)])


def shift_x(v, by):
    return lax.ppermute(v, "x", [(i, (i + by) % NX) for i in range(NX)])


def ring_y(v):
    pairs = []
    for y in range(NY):
        pairs.append((y * NC, (y + 1) % NY * NC))
        pairs.append((y * NC + 1, (y - 1) % NY * NC + 1))
    return lax.ppermute(v, ("y", "core"), pairs)


def row_order(first_half):
    y, core = lax.axis_index("y"), lax.axis_index("core")
    i = lax.broadcasted_iota(jnp.int32, (SEQ_LEN, SEQ_LEN), 0)
    j = lax.broadcasted_iota(jnp.int32, (SEQ_LEN, SEQ_LEN), 1)
    half, t, r = i // (NY * BLK), (i // BLK) % NY, i % BLK
    sign = jnp.where((core + half) % 2 == 0, 1, -1)
    block = (y - sign * t + NY) % NY
    source = ((first_half + half) % 2) * (NY * BLK) + block * BLK + r
    return (source == j).astype(BF)


def reorder(v, first_half):
    return jnp.dot(row_order(first_half), v, preferred_element_type=F32).astype(BF)


def rotate_chunk(rows, basis):
    n = len(rows)
    k = rows[0].shape[1]
    lhs = jnp.concatenate(rows, axis=0) if n > 1 else rows[0]
    part = jnp.dot(lhs, basis, preferred_element_type=F32)
    width = part.shape[1]
    part = part.reshape(n, NC, NY, BLK, width)
    keep = part[:, 0] + swap(part[:, 1].astype(BF), "core").astype(F32)
    total = keep[:, 1]
    for t in range(2, NY + 1):
        total = ring_y(total.astype(BF)).astype(F32) + keep[:, t % NY]
    total = total + swap(total.astype(BF), "zh").astype(F32)
    pieces = [total.astype(BF)]
    for _ in range(NY - 1):
        pieces.append(ring_y(pieces[-1]))
    own = jnp.stack(pieces, axis=1).reshape(n, NY * BLK, width)
    return own, swap(own, "core")


def rotate_inputs(layer_inputs, basis):
    x, zl = lax.axis_index("x"), lax.axis_index("zl")
    y, zh, core = lax.axis_index("y"), lax.axis_index("zh"), lax.axis_index("core")
    channels = layer_inputs.shape[1]
    step = jnp.stack([layer_inputs, swap(layer_inputs, "zh")])
    steps = [step]
    for _ in range(NY - 1):
        steps.append(ring_y(steps[-1]))
    own = jnp.stack(steps)
    other = swap(own, "core")
    other = jnp.stack([other[0], other[3], other[2], other[1]])
    rows = jnp.concatenate([own, other], axis=2).reshape(-1, channels)
    part = jnp.dot(rows, basis, preferred_element_type=F32)
    width = part.shape[1]
    part = part.reshape(NY, NZH, SEQ_LEN, width)
    sign = jnp.where(core == 0, 1, -1)

    def of_x(xx):
        t = (sign * (y - xx) + 2 * NY) % NY
        return lax.dynamic_index_in_dim(part, t, 0, keepdims=False)

    total = (
        of_x(x)
        + shift_x(of_x((x + 1) % NX), 1)
        + shift_x(of_x((x + 3) % NX), -1)
        + shift_x(of_x((x + 2) % NX), 2)
    )
    flip = zl ^ zh
    mine = lax.dynamic_index_in_dim(total, flip, 0, keepdims=False)
    theirs = lax.dynamic_index_in_dim(total, 1 - flip, 0, keepdims=False)
    mine = (mine + swap(theirs, "zl")).astype(BF)
    mine = reorder(mine, 0)
    pair = jnp.stack([mine, swap(mine, "zl")])
    before, after, far = shift_x(pair, 1), shift_x(pair, -1), shift_x(pair, 2)
    return jnp.stack([pair[0], pair[1], before[0], after[0], before[1], after[1], far[0], far[1]])


def square_kernel(sizes, *refs):
    x_ref, out_ref = refs[-2], refs[-1]
    s = 0
    for c, n in enumerate(sizes):
        own, other = refs[2 * c], refs[2 * c + 1]
        for i in range(n):
            g = jnp.concatenate([own[i], other[i]], axis=0)
            p = lax.dot_general(g, x_ref[s], (((0,), (0,)), ((), ())), preferred_element_type=F32)
            if s == 0:
                out_ref[...] = p * p
            else:
                out_ref[...] += p * p
            s += 1
    out_ref[...] *= 1.0 / s


def square_sum(chunks, inputs):
    sizes = tuple(own.shape[0] for own, _ in chunks)
    rows = chunks[0][0].shape[2]
    cols = inputs.shape[2]
    tile = 512
    specs = []
    operands = []
    for own, other in chunks:
        for v in (own, other):
            specs.append(pl.BlockSpec((v.shape[0], v.shape[1], tile), lambda i: (0, 0, i)))
            operands.append(v)
    specs.append(pl.BlockSpec(inputs.shape, lambda i: (0, 0, 0)))
    return pl.pallas_call(
        lambda *refs: square_kernel(sizes, *refs),
        grid=(rows // tile,),
        in_specs=specs,
        out_specs=pl.BlockSpec((tile, cols), lambda i: (i, 0)),
        out_shape=jax.ShapeDtypeStruct((rows, cols), F32),
        compiler_params=pltpu.CompilerParams(vmem_limit_bytes=32 * 1024 * 1024),
        cost_estimate=pl.CostEstimate(
            flops=2 * sum(sizes) * SEQ_LEN * rows * cols, bytes_accessed=rows * cols * 4, transcendentals=0
        ),
    )(*operands, inputs)


def body(out_grads, layer_inputs, basis_out, basis_in):
    core = lax.axis_index("core")
    own = reorder(out_grads, core)
    near = swap(own, "zl")
    before, after = shift_x(own, 1), shift_x(own, -1)
    before_n, after_n = shift_x(near, 1), shift_x(near, -1)
    h = SEQ_LEN // 2
    far = jnp.concatenate([shift_x(before[:h], 1), shift_x(after[h:], -1)], axis=0)
    far_n = jnp.concatenate([shift_x(before_n[:h], 1), shift_x(after_n[h:], -1)], axis=0)
    inputs = rotate_inputs(layer_inputs, basis_in)
    chunks = [
        rotate_chunk(rows, basis_out)
        for rows in ([own], [near, before, after], [before_n, after_n], [far, far_n])
    ]
    return square_sum(chunks, inputs)


def solution(mesh):
    fine = Mesh(mesh.devices.reshape(NX, NZL, NY, NZH, NC), ("x", "zl", "y", "zh", "core"))
    out, inn = ("x", "zl"), ("y", "zh", "core")
    return jax.shard_map(
        body,
        mesh=fine,
        in_specs=(P(out, inn), P(inn, out), P(inn, out), P(out, inn)),
        out_specs=P(out, inn),
        check_vma=False,
    )
```

```python
import jax
import jax.numpy as jnp
from jax import lax
from jax.experimental import pallas as pl
from jax.experimental.pallas import tpu as pltpu
from jax.sharding import Mesh
from jax.sharding import PartitionSpec as P

SEQ_LEN = 128
NX, NZL, NY, NZH, NC = 4, 2, 4, 2, 2
BLK = SEQ_LEN // (NY * NC)
BF = jnp.bfloat16
F32 = jnp.float32


def swap(v, axis):
    return lax.ppermute(v, axis, [(0, 1), (1, 0)])


def shift_x(v, by):
    return lax.ppermute(v, "x", [(i, (i + by) % NX) for i in range(NX)])


def near_bit():
    return jnp.where(lax.axis_index("core") == 0, 1, 3)


def trade(v, axis, other=False):
    pairs = []
    for i in range(4):
        for core, bit in ((0, 1), (1, 3)):
            pairs.append((i * NC + core, (i ^ (4 - bit if other else bit)) * NC + core))
    return lax.ppermute(v, (axis, "core"), pairs)


def pick(v, index, axis):
    return lax.dynamic_index_in_dim(v, index, axis, keepdims=False)


class Line:
    def __init__(self):
        self.last = ()

    def run(self, step, *operands):
        result = step(*lax.optimization_barrier(operands + self.last)[: len(operands)])
        self.last = tuple(result) if isinstance(result, (tuple, list)) else (result,)
        return result

    def put(self, v):
        return self.run(lambda u: u, v)


def reorder(v):
    y, a = lax.axis_index("y"), near_bit()
    i = lax.broadcasted_iota(jnp.int32, (SEQ_LEN, SEQ_LEN), 0)
    j = lax.broadcasted_iota(jnp.int32, (SEQ_LEN, SEQ_LEN), 1)
    half, t, r = i // (NY * BLK), (i // BLK) % NY, i % BLK
    bit = jnp.where(t == 0, 0, jnp.where(t == 3, 2, jnp.where(t == 1 + half, 4 - a, a)))
    hot = (half * (NY * BLK) + (y ^ bit) * BLK + r == j).astype(BF)
    return jnp.einsum("ij,njk->nik", hot, v, preferred_element_type=F32).astype(BF)


class Chunk:
    def __init__(self, line, basis):
        self.line, self.basis = line, basis

    def multiply(self, join, *received):
        def step(*received):
            lhs = join(*received)
            part = jnp.dot(lhs, self.basis, preferred_element_type=F32)
            part = part.reshape(lhs.shape[0] // SEQ_LEN, NC, NY, BLK, part.shape[1])
            core = lax.axis_index("core")
            return pick(part, 1 - core, 1).astype(BF), pick(part, core, 1)

        self.send, self.mine = self.line.run(step, *received)

    def cross(self):
        self.theirs = swap(self.send, "core")

    def blocks(self):
        y, a = lax.axis_index("y"), near_bit()

        def step(mine, theirs):
            def block(bit):
                return pick(mine, y ^ bit, 1) + pick(theirs, y ^ bit, 1).astype(F32)

            send = jnp.stack([block(a).astype(BF), block(2).astype(BF)])
            return send, block(0), block(4 - a)

        send, self.here, self.next = self.line.run(step, self.mine, self.theirs)
        self.r = trade(send, "y")

    def reduce(self):
        def step(here, next_, r):
            return (next_ + r[1].astype(F32)).astype(BF), here + r[0].astype(F32)

        send, self.here = self.line.run(step, self.here, self.next, self.r)
        self.r = trade(send, "y", other=True)

    def exchange(self):
        def step(here, r):
            total = here + r.astype(F32)
            return total.astype(BF), total

        send, self.here = self.line.run(step, self.here, self.r)
        self.r = swap(send, "zh")

    def gather(self):
        self.g = self.line.run(lambda u, v: (u + v.astype(F32)).astype(BF), self.here, self.r)
        self.r = trade(self.g, "y", other=True)

    def gather_more(self):
        self.g = self.line.run(lambda u, v: jnp.stack([u, v]), self.g, self.r)
        self.r = trade(self.g, "y")

    def cross_back(self):
        def step(u, v):
            own = jnp.concatenate([u, v], axis=0).swapaxes(0, 1)
            return own.reshape(own.shape[0], NY * BLK, own.shape[-1])

        self.own = self.line.run(step, self.g, self.r)
        self.other = swap(self.own, "core")


class Inputs:
    def __init__(self, line, basis):
        self.line, self.basis = line, basis

    def rows(self, rows):
        self.g = rows
        self.r = trade(rows, "y", other=True)

    def rows_more(self):
        self.g = self.line.run(lambda u, v: jnp.stack([u, v]), self.g, self.r)
        self.r = trade(self.g, "y")

    def rows_z(self):
        self.g = self.line.run(lambda u, v: jnp.concatenate([u, v], axis=0), self.g, self.r)
        self.r = swap(self.g, "zh")

    def rows_cross(self):
        self.g = self.line.run(lambda u, v: jnp.stack([u, v]), self.g, self.r)
        self.r = swap(self.g, "core")

    def multiply(self):
        def step(own, other):
            other = jnp.stack([other[:, t] for t in (0, 2, 1, 3)], axis=1)
            rows = jnp.concatenate([own, other], axis=2).reshape(-1, own.shape[-1])
            part = jnp.dot(rows, self.basis, preferred_element_type=F32)
            return part.reshape(NZH, NY, SEQ_LEN, part.shape[1])

        self.part = self.line.run(step, self.g, self.r)

    def block(self, part, bit):
        off = lax.axis_index("y") ^ lax.axis_index("x") ^ bit
        t = jnp.where(off == 0, 0, jnp.where(off == 2, 3, jnp.where(off == near_bit(), 2, 1)))
        return pick(part, t, 1)

    def reduce(self):
        a = near_bit()

        def step(p):
            return jnp.stack([self.block(p, a), self.block(p, 2)]), self.block(p, 0), self.block(p, 4 - a)

        send, self.here, self.next = self.line.run(step, self.part)
        self.r = trade(send, "x")

    def reduce_more(self):
        def step(here, next_, r):
            return next_ + r[1], here + r[0]

        send, self.here = self.line.run(step, self.here, self.next, self.r)
        self.r = trade(send, "x", other=True)

    def exchange(self):
        self.here = self.line.run(lambda u, v: u + v, self.here, self.r)
        self.r = swap(self.here, "zl")

    def gather(self):
        flip = lax.axis_index("zl") ^ lax.axis_index("zh")

        def step(u, v):
            total = (u + v).astype(BF)
            return reorder(jnp.stack([pick(total, flip, 0), pick(total, 1 - flip, 0)]))

        self.g = self.line.run(step, self.here, self.r)
        self.r = trade(self.g, "x", other=True)

    def gather_more(self):
        self.g = self.line.run(lambda u, v: jnp.stack([u, v]), self.g, self.r)
        self.r = trade(self.g, "x")

    def all(self):
        straight = (lax.axis_index("x") + lax.axis_index("core")) % 2 == 0

        def step(g, r):
            before, after = jnp.where(straight, g[1], r[0]), jnp.where(straight, r[0], g[1])
            return jnp.stack(
                [g[0, 0], g[0, 1], before[0], after[0], before[1], after[1], r[1, 0], r[1, 1]]
            )

        return self.line.run(step, self.g, self.r)


def square_kernel(sizes, *refs):
    x_ref, out_ref = refs[-2], refs[-1]
    s = 0
    for c, n in enumerate(sizes):
        own, other = refs[2 * c], refs[2 * c + 1]
        for i in range(n):
            g = jnp.concatenate([own[i], other[i]], axis=0)
            p = lax.dot_general(g, x_ref[s], (((0,), (0,)), ((), ())), preferred_element_type=F32)
            if s == 0:
                out_ref[...] = p * p
            else:
                out_ref[...] += p * p
            s += 1
    out_ref[...] *= 1.0 / s


def square_sum(chunks, inputs):
    sizes = tuple(own.shape[0] for own, _ in chunks)
    rows = chunks[0][0].shape[2]
    cols = inputs.shape[2]
    tile = 512
    specs = []
    operands = []
    for own, other in chunks:
        for v in (own, other):
            specs.append(pl.BlockSpec((v.shape[0], v.shape[1], tile), lambda i: (0, 0, i)))
            operands.append(v)
    specs.append(pl.BlockSpec(inputs.shape, lambda i: (0, 0, 0)))
    return pl.pallas_call(
        lambda *refs: square_kernel(sizes, *refs),
        grid=(rows // tile,),
        in_specs=specs,
        out_specs=pl.BlockSpec((tile, cols), lambda i: (i, 0)),
        out_shape=jax.ShapeDtypeStruct((rows, cols), F32),
        compiler_params=pltpu.CompilerParams(vmem_limit_bytes=32 * 1024 * 1024),
        cost_estimate=pl.CostEstimate(
            flops=2 * sum(sizes) * SEQ_LEN * rows * cols, bytes_accessed=rows * cols * 4, transcendentals=0
        ),
    )(*operands, inputs)


def body(out_grads, layer_inputs, basis_out, basis_in):
    line = Line()
    one, two, three = (Chunk(line, basis_out) for _ in range(3))
    inputs = Inputs(line, basis_in)
    half = SEQ_LEN // 2

    def join(*rows):
        return jnp.concatenate(rows, axis=0)

    def join_far(low, high):
        return jnp.concatenate([low, high], axis=1).reshape(-1, low.shape[-1])

    near = swap(out_grads, "zl")
    before, after = shift_x(out_grads, 1), shift_x(out_grads, -1)
    inputs.rows(layer_inputs)
    inputs.rows_more()
    near = line.put(near)
    before_n, after_n = shift_x(near, 1), shift_x(near, -1)
    one.multiply(join, out_grads, near, before, after)
    inputs.rows_z()
    one.cross()
    low = shift_x(line.run(lambda u, v: jnp.stack([u[:half], v[:half]]), before, before_n), 1)
    high = shift_x(line.run(lambda u, v: jnp.stack([u[half:], v[half:]]), after, after_n), -1)
    two.multiply(join, before_n, after_n)
    two.cross()
    one.blocks()
    inputs.rows_cross()
    two.blocks()
    three.multiply(join_far, low, high)
    three.cross()
    inputs.multiply()
    inputs.reduce()
    one.reduce()
    three.blocks()
    two.reduce()
    one.exchange()
    inputs.reduce_more()
    three.reduce()
    two.exchange()
    inputs.exchange()
    three.exchange()
    one.gather()
    two.gather()
    inputs.gather()
    three.gather()
    one.gather_more()
    inputs.gather_more()
    two.gather_more()
    three.gather_more()
    one.cross_back()
    two.cross_back()
    x_rows = inputs.all()
    three.cross_back()
    return square_sum([(c.own, c.other) for c in (one, two, three)], x_rows)


def solution(mesh):
    fine = Mesh(mesh.devices.reshape(NX, NZL, NY, NZH, NC), ("x", "zl", "y", "zh", "core"))
    out, inn = ("x", "zl"), ("y", "zh", "core")
    return jax.shard_map(
        body,
        mesh=fine,
        in_specs=(P(out, inn), P(inn, out), P(inn, out), P(out, inn)),
        out_specs=P(out, inn),
        check_vma=False,
    )
```

```python
import jax
import jax.numpy as jnp
from jax import lax
from jax.experimental import pallas as pl
from jax.experimental.pallas import tpu as pltpu
from jax.sharding import Mesh
from jax.sharding import PartitionSpec as P

SEQ_LEN = 128
NX, NZL, NY, NZH, NC = 4, 2, 4, 2, 2
BLK = SEQ_LEN // (NY * NC)
BF = jnp.bfloat16
F32 = jnp.float32


def swap(v, axis):
    return lax.ppermute(v, axis, [(0, 1), (1, 0)])


def shift_x(v, by):
    return lax.ppermute(v, "x", [(i, (i + by) % NX) for i in range(NX)])


def near_bit():
    return jnp.where(lax.axis_index("core") == 0, 1, 3)


def trade(v, axis, other=False):
    pairs = []
    for i in range(4):
        for core, bit in ((0, 1), (1, 3)):
            pairs.append((i * NC + core, (i ^ (4 - bit if other else bit)) * NC + core))
    return lax.ppermute(v, (axis, "core"), pairs)


def pick(v, index, axis):
    return lax.dynamic_index_in_dim(v, index, axis, keepdims=False)


class Line:
    def __init__(self):
        self.last = ()

    def run(self, step, received, *at_hand):
        received = lax.optimization_barrier((received,) + self.last)[0]
        result = step(received, *at_hand)
        self.last = (result[0] if isinstance(result, tuple) else result,)
        return result

    def put(self, v):
        return self.run(lambda u: u, v)


def order_matrix(half, block):
    i = lax.broadcasted_iota(jnp.int32, (SEQ_LEN, SEQ_LEN), 0)
    j = lax.broadcasted_iota(jnp.int32, (SEQ_LEN, SEQ_LEN), 1)
    h, t, r = i // (NY * BLK), (i // BLK) % NY, i % BLK
    return (half(h) * (NY * BLK) + block(h, t) * BLK + r == j).astype(BF)


def bit_of(t, first, second):
    return jnp.where(t == 0, 0, jnp.where(t == 3, 2, jnp.where(t == 1, first, second)))


def to_send_order(v):
    y, a, core = lax.axis_index("y"), near_bit(), lax.axis_index("core")

    def block(h, t):
        ha = jnp.where(h == 0, 4 - a, a)
        return y ^ bit_of((t + 2) % NY, 4 - ha, ha)

    hot = order_matrix(lambda h: (core + 1 + h) % 2, block)
    return jnp.dot(hot, v, preferred_element_type=F32).astype(BF)


def to_gather_order(v):
    y, a = lax.axis_index("y"), near_bit()

    def block(h, t):
        ha = jnp.where(h == 0, a, 4 - a)
        return y ^ bit_of(t, 4 - ha, ha)

    hot = order_matrix(lambda h: h, block)
    return jnp.einsum("ij,njk->nik", hot, v, preferred_element_type=F32).astype(BF)


def to_blocks(rows):
    k = rows[0].shape[-1]
    return jnp.stack([v.reshape(NC, NY, BLK, k) for v in rows], axis=2).reshape(NC, -1, k)


class Chunk:
    def __init__(self, line, basis, n):
        self.line, self.basis, self.n = line, basis, n

    def dot(self, rows):
        return jnp.dot(rows, self.basis, preferred_element_type=F32)

    def shape(self, v):
        return v.reshape(-1, self.n, BLK, v.shape[-1])

    def multiply(self, join, received, *at_hand):
        def step(received, *at_hand):
            rows = to_blocks(join(received, *at_hand))
            if self.n > 2:
                return self.dot(rows[0]).astype(BF), rows[1]
            part = self.dot(rows.reshape(-1, rows.shape[-1]))
            half = part.shape[0] // 2
            return part[:half].astype(BF), part[half:]

        send, self.mine = self.line.run(step, received, *at_hand)
        self.r = swap(self.shape(send), "core")
        if self.n > 2:
            self.mine = self.line.run(self.dot, self.mine)
        self.mine = self.shape(self.mine)

    def blocks(self):
        def step(r, mine):
            return (mine[:2] + r[:2].astype(F32)).astype(BF), mine[2:] + r[2:].astype(F32)

        send, self.here = self.line.run(step, self.r, self.mine)
        self.r = trade(send, "y")

    def reduce(self):
        def step(r, here):
            return (here[1] + r[1].astype(F32)).astype(BF), here[0] + r[0].astype(F32)

        send, self.here = self.line.run(step, self.r, self.here)
        self.r = trade(send, "y", other=True)

    def exchange(self):
        def step(r, here):
            total = here + r.astype(F32)
            return total.astype(BF), total

        send, self.here = self.line.run(step, self.r, self.here)
        self.r = swap(send, "zh")

    def gather(self):
        self.g = self.line.run(lambda r, u: (u + r.astype(F32)).astype(BF), self.r, self.here)
        self.r = trade(self.g, "y", other=True)

    def gather_more(self):
        self.g = self.line.run(lambda r, u: jnp.stack([u, r]), self.r, self.g)
        self.r = trade(self.g, "y")

    def cross_back(self):
        def step(r, u):
            own = jnp.concatenate([u, r], axis=0).swapaxes(0, 1)
            return own.reshape(own.shape[0], NY * BLK, own.shape[-1])

        self.own = self.line.run(step, self.r, self.g)
        self.other = swap(self.own, "core")


def part_kernel(own_at, other_at, own, other, basis, out):
    rows = jnp.concatenate([own[0, 0], other[0, 0], own[1, 0], other[1, 0]], axis=0)
    part = jnp.dot(rows, basis[...], preferred_element_type=F32)
    out[...] = part.reshape(out.shape)


def part_sums(own_at, other_at, own, other, basis):
    steps, (k, width) = own_at.shape[0], basis.shape
    block = (NZH, 1) + own.shape[2:]
    return pl.pallas_call(
        part_kernel,
        grid_spec=pltpu.PrefetchScalarGridSpec(
            num_scalar_prefetch=2,
            grid=(steps,),
            in_specs=[
                pl.BlockSpec(block, lambda i, own_at, other_at: (0, own_at[i], 0, 0)),
                pl.BlockSpec(block, lambda i, own_at, other_at: (0, other_at[i], 0, 0)),
                pl.BlockSpec((k, width), lambda i, own_at, other_at: (0, 0)),
            ],
            out_specs=pl.BlockSpec((1, NZH, SEQ_LEN, width), lambda i, own_at, other_at: (i, 0, 0, 0)),
        ),
        out_shape=jax.ShapeDtypeStruct((steps, NZH, SEQ_LEN, width), F32),
        compiler_params=pltpu.CompilerParams(vmem_limit_bytes=16 * 1024 * 1024),
        cost_estimate=pl.CostEstimate(
            flops=2 * steps * NZH * SEQ_LEN * k * width, bytes_accessed=k * width * 2, transcendentals=0
        ),
    )(own_at, other_at, own, other, basis)


class Inputs:
    def __init__(self, line, basis):
        self.line, self.basis = line, basis

    def rows(self, rows):
        self.g = rows
        self.r = trade(rows, "y", other=True)

    def rows_more(self):
        self.g = self.line.run(lambda r, u: jnp.stack([u, r]), self.r, self.g)
        self.r = trade(self.g, "y")

    def rows_z(self):
        self.g = self.line.run(lambda r, u: jnp.concatenate([u, r], axis=0), self.r, self.g)
        self.r = swap(self.g, "zh")

    def rows_cross(self):
        self.g = self.line.run(lambda r, u: jnp.stack([u, r]), self.r, self.g)
        self.r = swap(self.g, "core")

    def multiply(self):
        a = near_bit()
        off = lax.axis_index("y") ^ lax.axis_index("x")

        def at(bits, b):
            bits = jnp.stack([off ^ bit for bit in bits])
            return jnp.where(bits == 0, 0, jnp.where(bits == 2, 3, jnp.where(bits == b, 1, 2)))

        def step(r, g, bits):
            return part_sums(at(bits, 4 - a), at(bits, a), g, r, self.basis)

        send = self.line.run(lambda r, g: step(r, g, (a, 2)), self.r, self.g)
        other = self.r
        self.r = trade(send, "x")
        self.here = self.line.run(lambda r, g: step(r, g, (0, 4 - a)), other, self.g)

    def reduce(self):
        send, self.here = self.line.run(lambda r, u: (u[1] + r[1], u[0] + r[0]), self.r, self.here)
        self.r = trade(send, "x", other=True)

    def exchange(self):
        self.here = self.line.run(lambda r, u: u + r, self.r, self.here)
        self.r = swap(self.here, "zl")

    def gather(self):
        flip = lax.axis_index("zl") ^ lax.axis_index("zh")

        def step(r, u):
            total = (u + r).astype(BF)
            return to_gather_order(jnp.stack([pick(total, flip, 0), pick(total, 1 - flip, 0)]))

        self.g = self.line.run(step, self.r, self.here)
        self.r = trade(self.g, "x", other=True)

    def gather_more(self):
        self.g = self.line.run(lambda r, u: jnp.stack([u, r]), self.r, self.g)
        self.r = trade(self.g, "x")

    def all(self):
        straight = (lax.axis_index("x") + lax.axis_index("core")) % 2 == 0

        def step(r, g):
            before, after = jnp.where(straight, g[1], r[0]), jnp.where(straight, r[0], g[1])
            return jnp.stack(
                [g[0, 0], g[0, 1], before[0], after[0], before[1], after[1], r[1, 0], r[1, 1]]
            )

        return self.line.run(step, self.r, self.g)


def square_kernel(sizes, *refs):
    x_ref, out_ref = refs[-2], refs[-1]
    s = 0
    for c, n in enumerate(sizes):
        own, other = refs[2 * c], refs[2 * c + 1]
        for i in range(n):
            g = jnp.concatenate([own[i], other[i]], axis=0)
            p = lax.dot_general(g, x_ref[s], (((0,), (0,)), ((), ())), preferred_element_type=F32)
            if s == 0:
                out_ref[...] = p * p
            else:
                out_ref[...] += p * p
            s += 1
    out_ref[...] *= 1.0 / s


def square_sum(chunks, inputs):
    sizes = tuple(own.shape[0] for own, _ in chunks)
    rows = chunks[0][0].shape[2]
    cols = inputs.shape[2]
    tile = 512
    specs = []
    operands = []
    for own, other in chunks:
        for v in (own, other):
            specs.append(pl.BlockSpec((v.shape[0], v.shape[1], tile), lambda i: (0, 0, i)))
            operands.append(v)
    specs.append(pl.BlockSpec(inputs.shape, lambda i: (0, 0, 0)))
    return pl.pallas_call(
        lambda *refs: square_kernel(sizes, *refs),
        grid=(rows // tile,),
        in_specs=specs,
        out_specs=pl.BlockSpec((tile, cols), lambda i: (i, 0)),
        out_shape=jax.ShapeDtypeStruct((rows, cols), F32),
        compiler_params=pltpu.CompilerParams(vmem_limit_bytes=32 * 1024 * 1024),
        cost_estimate=pl.CostEstimate(
            flops=2 * sum(sizes) * SEQ_LEN * rows * cols, bytes_accessed=rows * cols * 4, transcendentals=0
        ),
    )(*operands, inputs)


def body(out_grads, layer_inputs, basis_out, basis_in):
    line = Line()
    one, two, three = (Chunk(line, basis_out, n) for n in (4, 2, 2))
    inputs = Inputs(line, basis_in)
    half = SEQ_LEN // 2

    inputs.rows(layer_inputs)
    own = to_send_order(out_grads)
    near = swap(own, "zl")
    before, after = shift_x(own, 1), shift_x(own, -1)
    inputs.rows_more()
    near = line.put(near)
    before_n, after_n = shift_x(near, 1), shift_x(near, -1)
    one.multiply(lambda u, *v: [own, near, *v, u], after, before)
    inputs.rows_z()
    one.blocks()
    low = shift_x(line.run(lambda v, u: jnp.stack([u[:half], v[:half]]), before_n, before), 1)
    high = shift_x(line.run(lambda v, u: jnp.stack([u[half:], v[half:]]), after_n, after), -1)
    two.multiply(lambda u, v: [u, v], before_n, after_n)
    inputs.rows_cross()
    two.blocks()
    inputs.multiply()
    three.multiply(lambda v, u: list(jnp.concatenate([u, v], axis=1)), high, low)
    one.reduce()
    three.blocks()
    two.reduce()
    one.exchange()
    inputs.reduce()
    three.reduce()
    two.exchange()
    one.gather()
    inputs.exchange()
    three.exchange()
    two.gather()
    one.gather_more()
    inputs.gather()
    three.gather()
    two.gather_more()
    inputs.gather_more()
    one.cross_back()
    three.gather_more()
    two.cross_back()
    x_rows = inputs.all()
    three.cross_back()
    return square_sum([(c.own, c.other) for c in (one, two, three)], x_rows)


def solution(mesh):
    fine = Mesh(mesh.devices.reshape(NX, NZL, NY, NZH, NC), ("x", "zl", "y", "zh", "core"))
    out, inn = ("x", "zl"), ("y", "zh", "core")
    return jax.shard_map(
        body,
        mesh=fine,
        in_specs=(P(out, inn), P(inn, out), P(inn, out), P(out, inn)),
        out_specs=P(out, inn),
        check_vma=False,
    )
```

```python
import jax
import jax.numpy as jnp
from jax import lax
from jax.experimental import pallas as pl
from jax.experimental.pallas import tpu as pltpu
from jax.sharding import Mesh
from jax.sharding import PartitionSpec as P

SEQ_LEN = 128
NX, NZL, NY, NZH, NC = 4, 2, 4, 2, 2
BLK = SEQ_LEN // (NY * NC)
BF = jnp.bfloat16
F32 = jnp.float32


def swap(v, axis):
    return lax.ppermute(v, axis, [(0, 1), (1, 0)])


def near_bit():
    return jnp.where(lax.axis_index("core") == 0, 1, 3)


def trade(v, axis, other=False):
    pairs = []
    for i in range(4):
        for core, bit in ((0, 1), (1, 3)):
            pairs.append((i * NC + core, (i ^ (4 - bit if other else bit)) * NC + core))
    return lax.ppermute(v, (axis, "core"), pairs)


def pick(v, index, axis):
    return lax.dynamic_index_in_dim(v, index, axis, keepdims=False)


class Line:
    def __init__(self):
        self.last = ()

    def run(self, step, received, *at_hand):
        received = received if isinstance(received, tuple) else (received,)
        received = lax.optimization_barrier(received + self.last)[: len(received)]
        result = step(*received, *at_hand)
        self.last = (result[0] if isinstance(result, (tuple, list)) else result,)
        return result

    def put(self, v):
        return self.run(lambda u: u, v)


def order_matrix(half, block):
    i = lax.broadcasted_iota(jnp.int32, (SEQ_LEN, SEQ_LEN), 0)
    j = lax.broadcasted_iota(jnp.int32, (SEQ_LEN, SEQ_LEN), 1)
    h, t, r = i // (NY * BLK), (i // BLK) % NY, i % BLK
    return (half(h) * (NY * BLK) + block(h, t) * BLK + r == j).astype(BF)


def bit_of(t, first, second):
    return jnp.where(t == 0, 0, jnp.where(t == 3, 2, jnp.where(t == 1, first, second)))


def to_send_order(v):
    y, a, core = lax.axis_index("y"), near_bit(), lax.axis_index("core")

    def block(h, t):
        ha = jnp.where(h == 0, 4 - a, a)
        return y ^ bit_of((t + 2) % NY, 4 - ha, ha)

    hot = order_matrix(lambda h: (core + 1 + h) % 2, block)
    return jnp.dot(hot, v, preferred_element_type=F32).astype(BF)


def to_gather_order(v):
    y, a = lax.axis_index("y"), near_bit()

    def block(h, t):
        ha = jnp.where(h == 0, a, 4 - a)
        return y ^ bit_of(t, 4 - ha, ha)

    hot = order_matrix(lambda h: h, block)
    return jnp.einsum("ij,njk->nik", hot, v, preferred_element_type=F32).astype(BF)


def to_blocks(rows):
    k = rows[0].shape[-1]
    return jnp.stack([v.reshape(NC, NY, BLK, k) for v in rows], axis=2).reshape(NC, -1, k)


SPANS = 7


def rotate_kernel(rows, basis, *refs):
    have, outs = refs[:-2], refs[-2:]
    span, half = basis.shape[1] // SPANS, rows.shape[0] // 2
    for i in range(SPANS):
        at = pl.ds(i * span, span)
        part = jnp.dot(rows[...], basis[:, at], preferred_element_type=F32)
        for h, out in enumerate(outs):
            mine = part[h * half : (h + 1) * half].astype(out.dtype)
            if not have:
                out[:, at] = mine
                continue
            old, new, both = (v // NY for v in (have[h].shape[0], half, out.shape[0]))
            for t in range(NY):
                out[pl.ds(t * both, old), at] = have[h][pl.ds(t * old, old), at]
                out[pl.ds(t * both + old, new), at] = mine[t * new : (t + 1) * new]


def rotated(rows, basis, have=()):
    (m, k), n = rows.shape, basis.shape[1]
    height = m // 2 + (have[0].shape[0] if have else 0)
    vmem = pl.BlockSpec(memory_space=pltpu.VMEM)
    return pl.pallas_call(
        rotate_kernel,
        in_specs=[vmem] * (2 + len(have)),
        out_specs=[vmem] * 2,
        out_shape=[jax.ShapeDtypeStruct((height, n), t) for t in (BF, F32)],
        compiler_params=pltpu.CompilerParams(vmem_limit_bytes=8 * 1024 * 1024),
    )(rows, basis, *have)


class Chunk:
    def __init__(self, line, basis, n):
        self.line, self.basis, self.n, self.have = line, basis, n, ()

    def shape(self, v):
        return v.reshape(NY, -1, BLK, v.shape[-1])

    def multiply_own(self, rows):
        rows = to_blocks([rows]).reshape(-1, rows.shape[-1])
        self.have = self.line.run(lambda v: rotated(v, self.basis), rows)

    def multiply(self, join, *received):
        def step(*received):
            rows = to_blocks(join(*received))
            send, mine = rotated(rows.reshape(-1, rows.shape[-1]), self.basis, self.have)
            return self.shape(send), self.shape(mine)

        send, self.mine = self.line.run(step, received)
        self.r = swap(send, "core")

    def blocks(self):
        def step(r, mine):
            return (mine[:2] + r[:2].astype(F32)).astype(BF), mine[2:] + r[2:].astype(F32)

        send, self.here = self.line.run(step, self.r, self.mine)
        self.r = trade(send, "y")

    def reduce(self):
        def step(r, here):
            return (here[1] + r[1].astype(F32)).astype(BF), here[0] + r[0].astype(F32)

        send, self.here = self.line.run(step, self.r, self.here)
        self.r = trade(send, "y", other=True)

    def exchange(self):
        def step(r, here):
            total = here + r.astype(F32)
            return total.astype(BF), total

        send, self.here = self.line.run(step, self.r, self.here)
        self.r = swap(send, "zh")

    def gather(self):
        self.g = self.line.run(lambda r, u: (u + r.astype(F32)).astype(BF), self.r, self.here)
        self.r = trade(self.g, "y", other=True)

    def gather_more(self):
        self.g = self.line.run(lambda r, u: jnp.stack([u, r]), self.r, self.g)
        self.r = trade(self.g, "y")

    def cross_back(self):
        def step(r, u):
            own = jnp.concatenate([u, r], axis=0).swapaxes(0, 1)
            return own.reshape(own.shape[0], NY * BLK, own.shape[-1])

        self.own = self.line.run(step, self.r, self.g)
        self.other = swap(self.own, "core")


def part_kernel(own_at, other_at, own, other, basis, out):
    rows = jnp.concatenate([own[0, 0], other[0, 0], own[0, 1], other[0, 1]], axis=0)
    part = jnp.dot(rows, basis[...], preferred_element_type=F32)
    out[...] = part.reshape(out.shape)


def part_sums(own_at, other_at, own, other, basis):
    steps, (k, width) = own_at.shape[0], basis.shape
    block = (1,) + own.shape[1:]
    return pl.pallas_call(
        part_kernel,
        grid_spec=pltpu.PrefetchScalarGridSpec(
            num_scalar_prefetch=2,
            grid=(steps,),
            in_specs=[
                pl.BlockSpec(block, lambda i, own_at, other_at: (own_at[i], 0, 0, 0)),
                pl.BlockSpec(block, lambda i, own_at, other_at: (other_at[i], 0, 0, 0)),
                pl.BlockSpec((k, width), lambda i, own_at, other_at: (0, 0)),
            ],
            out_specs=pl.BlockSpec((1, NZH, SEQ_LEN, width), lambda i, own_at, other_at: (i, 0, 0, 0)),
        ),
        out_shape=jax.ShapeDtypeStruct((steps, NZH, SEQ_LEN, width), F32),
        compiler_params=pltpu.CompilerParams(vmem_limit_bytes=8 * 1024 * 1024),
        cost_estimate=pl.CostEstimate(
            flops=2 * steps * NZH * SEQ_LEN * k * width, bytes_accessed=k * width * 2, transcendentals=0
        ),
    )(own_at, other_at, own, other, basis)


class Inputs:
    def __init__(self, line, basis):
        self.line, self.basis = line, basis

    def rows(self, rows):
        self.g = rows
        self.r = trade(rows, "y", other=True)

    def rows_more(self):
        self.g = self.line.run(lambda r, u: jnp.stack([u, r]), self.r, self.g)
        self.r = trade(self.g, "y")

    def rows_z(self):
        self.g = self.line.run(lambda r, u: jnp.concatenate([u, r], axis=0), self.r, self.g)
        self.r = swap(self.g, "zh")

    def rows_cross(self):
        self.g = self.line.run(lambda r, u: jnp.stack([u, r], axis=1), self.r, self.g)
        self.r = swap(self.g, "core")

    def multiply(self):
        a = near_bit()
        off = lax.axis_index("y") ^ lax.axis_index("x")

        def at(bits, b):
            bits = jnp.stack([off ^ bit for bit in bits])
            return jnp.where(bits == 0, 0, jnp.where(bits == 2, 3, jnp.where(bits == b, 1, 2)))

        def step(r, g, bits):
            return part_sums(at(bits, 4 - a), at(bits, a), g, r, self.basis)

        send = self.line.run(lambda r, g: step(r, g, (a, 2)), self.r, self.g)
        other = self.r
        self.r = trade(send, "x")
        self.here = self.line.run(lambda r, g: step(r, g, (0, 4 - a)), other, self.g)

    def reduce(self):
        send, self.here = self.line.run(lambda r, u: (u[1] + r[1], u[0] + r[0]), self.r, self.here)
        self.r = trade(send, "x", other=True)

    def exchange(self):
        self.here = self.line.run(lambda r, u: u + r, self.r, self.here)
        self.r = swap(self.here, "zl")

    def gather(self):
        flip = lax.axis_index("zl") ^ lax.axis_index("zh")

        def step(r, u):
            total = (u + r).astype(BF)
            return to_gather_order(jnp.stack([pick(total, flip, 0), pick(total, 1 - flip, 0)]))

        self.g = self.line.run(step, self.r, self.here)
        self.r = trade(self.g, "x", other=True)

    def gather_more(self):
        self.g = self.line.run(lambda r, u: jnp.stack([u, r]), self.r, self.g)
        self.r = trade(self.g, "x")

    def all(self):
        straight = near_bit() == 1

        def step(r, g):
            one, three = jnp.where(straight, r[0], g[1]), jnp.where(straight, g[1], r[0])
            return jnp.stack([g[0, 0], g[0, 1], one[0], three[0], one[1], three[1], r[1, 0], r[1, 1]])

        return self.line.run(step, self.r, self.g)


def square_kernel(sizes, *refs):
    x_ref, out_ref = refs[-2], refs[-1]
    s = 0
    for c, n in enumerate(sizes):
        own, other = refs[2 * c], refs[2 * c + 1]
        for i in range(n):
            g = jnp.concatenate([own[i], other[i]], axis=0)
            p = lax.dot_general(g, x_ref[s], (((0,), (0,)), ((), ())), preferred_element_type=F32)
            if s == 0:
                out_ref[...] = p * p
            else:
                out_ref[...] += p * p
            s += 1
    out_ref[...] *= 1.0 / s


def square_sum(chunks, inputs):
    sizes = tuple(own.shape[0] for own, _ in chunks)
    rows = chunks[0][0].shape[2]
    cols = inputs.shape[2]
    tile = rows // 4
    specs = []
    operands = []
    for own, other in chunks:
        for v in (own, other):
            specs.append(pl.BlockSpec((v.shape[0], v.shape[1], tile), lambda i: (0, 0, i)))
            operands.append(v)
    specs.append(pl.BlockSpec(inputs.shape, lambda i: (0, 0, 0)))
    return pl.pallas_call(
        lambda *refs: square_kernel(sizes, *refs),
        grid=(rows // tile,),
        in_specs=specs,
        out_specs=pl.BlockSpec((tile, cols), lambda i: (i, 0)),
        out_shape=jax.ShapeDtypeStruct((rows, cols), F32),
        compiler_params=pltpu.CompilerParams(vmem_limit_bytes=20 * 1024 * 1024),
        cost_estimate=pl.CostEstimate(
            flops=2 * sum(sizes) * SEQ_LEN * rows * cols, bytes_accessed=rows * cols * 4, transcendentals=0
        ),
    )(*operands, inputs)


def body(out_grads, layer_inputs, basis_out, basis_in):
    line = Line()
    one, two, three = (Chunk(line, basis_out, n) for n in (4, 2, 2))
    inputs = Inputs(line, basis_in)
    half = SEQ_LEN // 2

    def by_bit(first, second):
        straight = near_bit() == 1
        return [jnp.where(straight, first, second), jnp.where(straight, second, first)]

    inputs.rows(layer_inputs)
    own = to_send_order(out_grads)
    near = swap(own, "zl")
    first, second = trade(own, "x"), trade(own, "x", other=True)
    one.multiply_own(own)
    inputs.rows_more()
    near = line.put(near)
    first_n, second_n = trade(near, "x"), trade(near, "x", other=True)
    one.multiply(lambda u, v: [near] + by_bit(u, v), first, second)
    inputs.rows_z()
    one.blocks()
    low = trade(line.run(lambda v, u: jnp.stack([u[:half], v[:half]]), second_n, second), "x")
    high = trade(line.run(lambda v, u: jnp.stack([u[half:], v[half:]]), first_n, first), "x", other=True)
    two.multiply(by_bit, first_n, second_n)
    inputs.rows_cross()
    one.reduce()
    two.blocks()
    inputs.multiply()
    three.multiply(lambda v, u: list(jnp.concatenate([u, v], axis=1)), high, low)
    one.exchange()
    three.blocks()
    two.reduce()
    inputs.reduce()
    three.reduce()
    two.exchange()
    one.gather()
    three.exchange()
    inputs.exchange()
    two.gather()
    one.gather_more()
    three.gather()
    two.gather_more()
    inputs.gather()
    three.gather_more()
    one.cross_back()
    inputs.gather_more()
    two.cross_back()
    three.cross_back()
    x_rows = inputs.all()
    return square_sum([(c.own, c.other) for c in (one, two, three)], x_rows)


def solution(mesh):
    fine = Mesh(mesh.devices.reshape(NX, NZL, NY, NZH, NC), ("x", "zl", "y", "zh", "core"))
    out, inn = ("x", "zl"), ("y", "zh", "core")
    return jax.shard_map(
        body,
        mesh=fine,
        in_specs=(P(out, inn), P(inn, out), P(inn, out), P(out, inn)),
        out_specs=P(out, inn),
        check_vma=False,
    )
```

```python
import functools

import jax
import jax.numpy as jnp
from jax import lax
from jax.experimental import pallas as pl
from jax.experimental.pallas import tpu as pltpu
from jax.sharding import Mesh
from jax.sharding import PartitionSpec as P

SEQ_LEN = 128
NX, NZL, NY, NZH, NC = 4, 2, 4, 2, 2
BLK = SEQ_LEN // (NY * NC)
BF = jnp.bfloat16
F32 = jnp.float32


def swap(v, axis):
    return lax.ppermute(v, axis, [(0, 1), (1, 0)])


def near_bit():
    return jnp.where(lax.axis_index("core") == 0, 1, 3)


def trade(v, axis, other=False):
    pairs = []
    for i in range(4):
        for core, bit in ((0, 1), (1, 3)):
            pairs.append((i * NC + core, (i ^ (4 - bit if other else bit)) * NC + core))
    return lax.ppermute(v, (axis, "core"), pairs)


def pick(v, index, axis):
    return lax.dynamic_index_in_dim(v, index, axis, keepdims=False)


class Line:
    def __init__(self):
        self.last = ()

    def run(self, step, received, *at_hand):
        received = received if isinstance(received, tuple) else (received,)
        received = lax.optimization_barrier(received + self.last)[: len(received)]
        result = step(*received, *at_hand)
        self.last = (result[0] if isinstance(result, (tuple, list)) else result,)
        return result

    def put(self, v):
        return self.run(lambda u: u, v)


def order_matrix(half, block):
    i = lax.broadcasted_iota(jnp.int32, (SEQ_LEN, SEQ_LEN), 0)
    j = lax.broadcasted_iota(jnp.int32, (SEQ_LEN, SEQ_LEN), 1)
    h, t, r = i // (NY * BLK), (i // BLK) % NY, i % BLK
    return (half(h) * (NY * BLK) + block(h, t) * BLK + r == j).astype(BF)


def bit_of(t, first, second):
    return jnp.where(t == 0, 0, jnp.where(t == 3, 2, jnp.where(t == 1, first, second)))


def to_send_order(v):
    y, a, core = lax.axis_index("y"), near_bit(), lax.axis_index("core")

    def block(h, t):
        ha = jnp.where(h == 0, 4 - a, a)
        return y ^ bit_of((t + 2) % NY, 4 - ha, ha)

    hot = order_matrix(lambda h: (core + 1 + h) % 2, block)
    return jnp.dot(hot, v, preferred_element_type=F32).astype(BF)


def to_gather_order(v):
    y, a = lax.axis_index("y"), near_bit()

    def block(h, t):
        ha = jnp.where(h == 0, a, 4 - a)
        return y ^ bit_of(t, 4 - ha, ha)

    hot = order_matrix(lambda h: h, block)
    return jnp.einsum("ij,njk->nik", hot, v, preferred_element_type=F32).astype(BF)


def to_blocks(rows):
    k = rows[0].shape[-1]
    return jnp.stack([v.reshape(NC, NY, BLK, k) for v in rows], axis=2).reshape(NC, -1, k)


SPANS = 7


def rotate_kernel(count, rows, basis, *refs):
    have, outs = refs[:-count], refs[-count:]
    span, height = basis.shape[1] // SPANS, rows.shape[0] // len(outs)
    for i in range(SPANS):
        at = pl.ds(i * span, span)
        part = jnp.dot(rows[...], basis[:, at], preferred_element_type=F32)
        for h, out in enumerate(outs):
            mine = part[h * height : (h + 1) * height].astype(out.dtype)
            if not have:
                out[:, at] = mine
                continue
            old, new, both = (v // NY for v in (have[h].shape[0], height, out.shape[0]))
            for t in range(NY):
                out[pl.ds(t * both, old), at] = have[h][pl.ds(t * old, old), at]
                out[pl.ds(t * both + old, new), at] = mine[t * new : (t + 1) * new]


def rotated(rows, basis, types, have=()):
    (m, k), n = rows.shape, basis.shape[1]
    height = m // len(types) + (have[0].shape[0] if have else 0)
    vmem = pl.BlockSpec(memory_space=pltpu.VMEM)
    return pl.pallas_call(
        functools.partial(rotate_kernel, len(types)),
        in_specs=[vmem] * (2 + len(have)),
        out_specs=[vmem] * len(types),
        out_shape=[jax.ShapeDtypeStruct((height, n), t) for t in types],
        compiler_params=pltpu.CompilerParams(vmem_limit_bytes=8 * 1024 * 1024),
    )(rows, basis, *have)


class Chunk:
    def __init__(self, line, basis, n):
        self.line, self.basis, self.n, self.have = line, basis, n, ()

    def shape(self, v):
        return v.reshape(NY, -1, BLK, v.shape[-1])

    def multiply_own(self, rows):
        rows = to_blocks([rows]).reshape(-1, rows.shape[-1])
        self.have = self.line.run(lambda v: rotated(v, self.basis, (BF, F32)), rows)

    def multiply(self, join, *received):
        def first(*received):
            rows = to_blocks(join(*received))
            return self.shape(rotated(rows[0], self.basis, (BF,), self.have[:1])[0]), rows[1]

        send, rows = self.line.run(first, received)
        self.r = swap(send, "core")
        last = self.line.last
        self.mine = self.line.run(
            lambda v: self.shape(rotated(v, self.basis, (F32,), self.have[1:])[0]), rows
        )
        self.line.last = last

    def blocks(self):
        def step(r, mine):
            return (mine[:2] + r[:2].astype(F32)).astype(BF), mine[2:] + r[2:].astype(F32)

        send, self.here = self.line.run(step, self.r, self.mine)
        self.r = trade(send, "y")

    def reduce(self):
        def step(r, here):
            return (here[1] + r[1].astype(F32)).astype(BF), here[0] + r[0].astype(F32)

        send, self.here = self.line.run(step, self.r, self.here)
        self.r = trade(send, "y", other=True)

    def exchange(self):
        def step(r, here):
            total = here + r.astype(F32)
            return total.astype(BF), total

        send, self.here = self.line.run(step, self.r, self.here)
        self.r = swap(send, "zh")

    def gather(self):
        self.g = self.line.run(lambda r, u: (u + r.astype(F32)).astype(BF), self.r, self.here)
        self.r = trade(self.g, "y", other=True)

    def gather_more(self):
        self.g = self.line.run(lambda r, u: jnp.stack([u, r]), self.r, self.g)
        self.r = trade(self.g, "y")

    def cross_back(self):
        def step(r, u):
            own = jnp.concatenate([u, r], axis=0).swapaxes(0, 1)
            return own.reshape(own.shape[0], NY * BLK, own.shape[-1])

        self.own = self.line.run(step, self.r, self.g)
        self.other = swap(self.own, "core")


def part_kernel(own_at, other_at, own, other, basis, out):
    rows = jnp.concatenate([own[0, 0], other[0, 0], own[0, 1], other[0, 1]], axis=0)
    part = jnp.dot(rows, basis[...], preferred_element_type=F32)
    out[...] = part.reshape(out.shape)


def part_sums(own_at, other_at, own, other, basis):
    steps, (k, width) = own_at.shape[0], basis.shape
    block = (1,) + own.shape[1:]
    return pl.pallas_call(
        part_kernel,
        grid_spec=pltpu.PrefetchScalarGridSpec(
            num_scalar_prefetch=2,
            grid=(steps,),
            in_specs=[
                pl.BlockSpec(block, lambda i, own_at, other_at: (own_at[i], 0, 0, 0)),
                pl.BlockSpec(block, lambda i, own_at, other_at: (other_at[i], 0, 0, 0)),
                pl.BlockSpec((k, width), lambda i, own_at, other_at: (0, 0)),
            ],
            out_specs=pl.BlockSpec((1, NZH, SEQ_LEN, width), lambda i, own_at, other_at: (i, 0, 0, 0)),
        ),
        out_shape=jax.ShapeDtypeStruct((steps, NZH, SEQ_LEN, width), F32),
        compiler_params=pltpu.CompilerParams(vmem_limit_bytes=8 * 1024 * 1024),
        cost_estimate=pl.CostEstimate(
            flops=2 * steps * NZH * SEQ_LEN * k * width, bytes_accessed=k * width * 2, transcendentals=0
        ),
    )(own_at, other_at, own, other, basis)


class Inputs:
    def __init__(self, line, basis):
        self.line, self.basis = line, basis

    def rows(self, rows):
        self.g = rows
        self.r = trade(rows, "y", other=True)

    def rows_more(self):
        self.g = self.line.run(lambda r, u: jnp.stack([u, r]), self.r, self.g)
        self.r = trade(self.g, "y")

    def rows_z(self):
        self.g = self.line.run(lambda r, u: jnp.concatenate([u, r], axis=0), self.r, self.g)
        self.r = swap(self.g, "zh")

    def rows_cross(self):
        self.g = self.line.run(lambda r, u: jnp.stack([u, r], axis=1), self.r, self.g)
        self.r = swap(self.g, "core")

    def multiply(self):
        a = near_bit()
        off = lax.axis_index("y") ^ lax.axis_index("x")

        def at(bits, b):
            bits = jnp.stack([off ^ bit for bit in bits])
            return jnp.where(bits == 0, 0, jnp.where(bits == 2, 3, jnp.where(bits == b, 1, 2)))

        def step(r, g, bits):
            return part_sums(at(bits, 4 - a), at(bits, a), g, r, self.basis)

        send = self.line.run(lambda r, g: step(r, g, (a, 2)), self.r, self.g)
        other = self.r
        self.r = trade(send, "x")
        self.here = self.line.run(lambda r, g: step(r, g, (0, 4 - a)), other, self.g)

    def reduce(self):
        send, self.here = self.line.run(lambda r, u: (u[1] + r[1], u[0] + r[0]), self.r, self.here)
        self.r = trade(send, "x", other=True)

    def exchange(self):
        self.here = self.line.run(lambda r, u: u + r, self.r, self.here)
        self.r = swap(self.here, "zl")

    def gather(self):
        flip = lax.axis_index("zl") ^ lax.axis_index("zh")

        def step(r, u):
            total = (u + r).astype(BF)
            return to_gather_order(jnp.stack([pick(total, flip, 0), pick(total, 1 - flip, 0)]))

        self.g = self.line.run(step, self.r, self.here)
        self.r = trade(self.g, "x", other=True)

    def gather_more(self):
        self.g = self.line.run(lambda r, u: jnp.stack([u, r]), self.r, self.g)
        self.r = trade(self.g, "x")

    def all(self):
        straight = near_bit() == 1

        def step(r, g):
            one, three = jnp.where(straight, r[0], g[1]), jnp.where(straight, g[1], r[0])
            return jnp.stack([g[0, 0], g[0, 1], one[0], three[0], one[1], three[1], r[1, 0], r[1, 1]])

        return self.line.run(step, self.r, self.g)


def square_kernel(sizes, *refs):
    x_ref, out_ref = refs[-2], refs[-1]
    s = 0
    for c, n in enumerate(sizes):
        own, other = refs[2 * c], refs[2 * c + 1]
        for i in range(n):
            g = jnp.concatenate([own[i], other[i]], axis=0)
            p = lax.dot_general(g, x_ref[s], (((0,), (0,)), ((), ())), preferred_element_type=F32)
            if s == 0:
                out_ref[...] = p * p
            else:
                out_ref[...] += p * p
            s += 1
    out_ref[...] *= 1.0 / s


def square_sum(chunks, inputs):
    sizes = tuple(own.shape[0] for own, _ in chunks)
    rows = chunks[0][0].shape[2]
    cols = inputs.shape[2]
    tile = rows // 4
    specs = []
    operands = []
    for own, other in chunks:
        for v in (own, other):
            specs.append(pl.BlockSpec((v.shape[0], v.shape[1], tile), lambda i: (0, 0, i)))
            operands.append(v)
    specs.append(pl.BlockSpec(inputs.shape, lambda i: (0, 0, 0)))
    return pl.pallas_call(
        lambda *refs: square_kernel(sizes, *refs),
        grid=(rows // tile,),
        in_specs=specs,
        out_specs=pl.BlockSpec((tile, cols), lambda i: (i, 0)),
        out_shape=jax.ShapeDtypeStruct((rows, cols), F32),
        compiler_params=pltpu.CompilerParams(vmem_limit_bytes=20 * 1024 * 1024),
        cost_estimate=pl.CostEstimate(
            flops=2 * sum(sizes) * SEQ_LEN * rows * cols, bytes_accessed=rows * cols * 4, transcendentals=0
        ),
    )(*operands, inputs)


def body(out_grads, layer_inputs, basis_out, basis_in):
    line = Line()
    one, two, three = (Chunk(line, basis_out, n) for n in (4, 2, 2))
    inputs = Inputs(line, basis_in)
    half = SEQ_LEN // 2

    def by_bit(first, second):
        straight = near_bit() == 1
        return [jnp.where(straight, first, second), jnp.where(straight, second, first)]

    inputs.rows(layer_inputs)
    own = to_send_order(out_grads)
    near = swap(own, "zl")
    first, second = trade(own, "x"), trade(own, "x", other=True)
    one.multiply_own(own)
    inputs.rows_more()
    near = line.put(near)
    first_n, second_n = trade(near, "x"), trade(near, "x", other=True)
    one.multiply(lambda u, v: [near] + by_bit(u, v), first, second)
    inputs.rows_z()
    one.blocks()
    low = trade(line.run(lambda v, u: jnp.stack([u[:half], v[:half]]), second_n, second), "x")
    high = trade(line.run(lambda v, u: jnp.stack([u[half:], v[half:]]), first_n, first), "x", other=True)
    two.multiply(by_bit, first_n, second_n)
    inputs.rows_cross()
    one.reduce()
    two.blocks()
    inputs.multiply()
    three.multiply(lambda v, u: list(jnp.concatenate([u, v], axis=1)), high, low)
    three.blocks()
    one.exchange()
    two.reduce()
    inputs.reduce()
    three.reduce()
    two.exchange()
    one.gather()
    three.exchange()
    inputs.exchange()
    two.gather()
    one.gather_more()
    three.gather()
    two.gather_more()
    inputs.gather()
    three.gather_more()
    one.cross_back()
    inputs.gather_more()
    two.cross_back()
    three.cross_back()
    x_rows = inputs.all()
    return square_sum([(c.own, c.other) for c in (one, two, three)], x_rows)


def solution(mesh):
    fine = Mesh(mesh.devices.reshape(NX, NZL, NY, NZH, NC), ("x", "zl", "y", "zh", "core"))
    out, inn = ("x", "zl"), ("y", "zh", "core")
    return jax.shard_map(
        body,
        mesh=fine,
        in_specs=(P(out, inn), P(inn, out), P(inn, out), P(out, inn)),
        out_specs=P(out, inn),
        check_vma=False,
    )
```

```python
import functools

import jax
import jax.numpy as jnp
from jax import lax
from jax.experimental import pallas as pl
from jax.experimental.pallas import tpu as pltpu
from jax.sharding import Mesh
from jax.sharding import PartitionSpec as P

SEQ_LEN = 128
NX, NZL, NY, NZH, NC = 4, 2, 4, 2, 2
BLK = SEQ_LEN // (NY * NC)
BF = jnp.bfloat16
F32 = jnp.float32


def swap(v, axis):
    return lax.ppermute(v, axis, [(0, 1), (1, 0)])


def near_bit():
    return jnp.where(lax.axis_index("core") == 0, 1, 3)


def trade(v, axis, other=False):
    pairs = []
    for i in range(4):
        for core, bit in ((0, 1), (1, 3)):
            pairs.append((i * NC + core, (i ^ (4 - bit if other else bit)) * NC + core))
    return lax.ppermute(v, (axis, "core"), pairs)


def pick(v, index, axis):
    return lax.dynamic_index_in_dim(v, index, axis, keepdims=False)


class Line:
    def __init__(self):
        self.last = ()

    def run(self, step, received, *at_hand):
        received = received if isinstance(received, tuple) else (received,)
        received = lax.optimization_barrier(received + self.last)[: len(received)]
        result = step(*received, *at_hand)
        self.last = (result[0] if isinstance(result, (tuple, list)) else result,)
        return result

    def put(self, v):
        return self.run(lambda u: u, v)


def order_matrix(half, block):
    i = lax.broadcasted_iota(jnp.int32, (SEQ_LEN, SEQ_LEN), 0)
    j = lax.broadcasted_iota(jnp.int32, (SEQ_LEN, SEQ_LEN), 1)
    h, t, r = i // (NY * BLK), (i // BLK) % NY, i % BLK
    return (half(h) * (NY * BLK) + block(h, t) * BLK + r == j).astype(BF)


def bit_of(t, first, second):
    return jnp.where(t == 0, 0, jnp.where(t == 3, 2, jnp.where(t == 1, first, second)))


def to_send_order(v):
    y, a, core = lax.axis_index("y"), near_bit(), lax.axis_index("core")

    def block(h, t):
        ha = jnp.where(h == 0, 4 - a, a)
        return y ^ bit_of((t + 2) % NY, 4 - ha, ha)

    hot = order_matrix(lambda h: (core + 1 + h) % 2, block)
    return jnp.dot(hot, v, preferred_element_type=F32).astype(BF)


def to_gather_order(v):
    y, a = lax.axis_index("y"), near_bit()

    def block(h, t):
        ha = jnp.where(h == 0, a, 4 - a)
        return y ^ bit_of(t, 4 - ha, ha)

    hot = order_matrix(lambda h: h, block)
    return jnp.einsum("ij,njk->nik", hot, v, preferred_element_type=F32).astype(BF)


def to_blocks(rows):
    k = rows[0].shape[-1]
    return jnp.stack([v.reshape(NC, NY, BLK, k) for v in rows], axis=2).reshape(NC, -1, k)


SPANS = 7


def rotate_kernel(count, rows, basis, *refs):
    have, outs = refs[:-count], refs[-count:]
    span, height = basis.shape[1] // SPANS, rows.shape[0] // len(outs)
    for i in range(SPANS):
        at = pl.ds(i * span, span)
        part = jnp.dot(rows[...], basis[:, at], preferred_element_type=F32)
        for h, out in enumerate(outs):
            mine = part[h * height : (h + 1) * height].astype(out.dtype)
            if not have:
                out[:, at] = mine
                continue
            old, new, both = (v // NY for v in (have[h].shape[0], height, out.shape[0]))
            for t in range(NY):
                out[pl.ds(t * both, old), at] = have[h][pl.ds(t * old, old), at]
                out[pl.ds(t * both + old, new), at] = mine[t * new : (t + 1) * new]


def rotated(rows, basis, types, have=()):
    (m, k), n = rows.shape, basis.shape[1]
    height = m // len(types) + (have[0].shape[0] if have else 0)
    vmem = pl.BlockSpec(memory_space=pltpu.VMEM)
    return pl.pallas_call(
        functools.partial(rotate_kernel, len(types)),
        in_specs=[vmem] * (2 + len(have)),
        out_specs=[vmem] * len(types),
        out_shape=[jax.ShapeDtypeStruct((height, n), t) for t in types],
        compiler_params=pltpu.CompilerParams(vmem_limit_bytes=8 * 1024 * 1024),
    )(rows, basis, *have)


class Chunk:
    def __init__(self, line, basis, n):
        self.line, self.basis, self.n, self.have = line, basis, n, ()

    def shape(self, v):
        return v.reshape(NY, -1, BLK, v.shape[-1])

    def multiply_own(self, rows):
        rows = to_blocks([rows]).reshape(-1, rows.shape[-1])
        self.have = self.line.run(lambda v: rotated(v, self.basis, (BF, F32)), rows)

    def multiply(self, join, *received):
        def first(*received):
            rows = to_blocks(join(*received))
            return self.shape(rotated(rows[0], self.basis, (BF,), self.have[:1])[0]), rows[1]

        send, rows = self.line.run(first, received)
        self.r = swap(send, "core")
        last = self.line.last
        self.mine = self.line.run(
            lambda v: self.shape(rotated(v, self.basis, (F32,), self.have[1:])[0]), rows
        )
        self.line.last = last

    def blocks(self):
        def step(r, mine):
            return (mine[:2] + r[:2].astype(F32)).astype(BF), mine[2:] + r[2:].astype(F32)

        send, self.here = self.line.run(step, self.r, self.mine)
        self.r = trade(send, "y")

    def reduce(self):
        def step(r, here):
            return (here[1] + r[1].astype(F32)).astype(BF), here[0] + r[0].astype(F32)

        send, self.here = self.line.run(step, self.r, self.here)
        self.r = trade(send, "y", other=True)

    def exchange(self):
        def step(r, here):
            total = here + r.astype(F32)
            return total.astype(BF), total

        send, self.here = self.line.run(step, self.r, self.here)
        self.r = swap(send, "zh")

    def gather(self):
        self.g = self.line.run(lambda r, u: (u + r.astype(F32)).astype(BF), self.r, self.here)
        self.r = trade(self.g, "y", other=True)

    def gather_more(self):
        self.g = self.line.run(lambda r, u: jnp.stack([u, r]), self.r, self.g)
        self.r = trade(self.g, "y")

    def cross_back(self):
        def step(r, u):
            own = jnp.concatenate([u, r], axis=0).swapaxes(0, 1)
            return own.reshape(own.shape[0], NY * BLK, own.shape[-1])

        self.own = self.line.run(step, self.r, self.g)
        self.other = swap(self.own, "core")


def part_kernel(own_at, other_at, own, other, basis, out):
    rows = jnp.concatenate([own[0, 0], other[0, 0], own[0, 1], other[0, 1]], axis=0)
    part = jnp.dot(rows, basis[...], preferred_element_type=F32)
    out[...] = part.reshape(out.shape)


def part_sums(own_at, other_at, own, other, basis):
    steps, (k, width) = own_at.shape[0], basis.shape
    block = (1,) + own.shape[1:]
    return pl.pallas_call(
        part_kernel,
        grid_spec=pltpu.PrefetchScalarGridSpec(
            num_scalar_prefetch=2,
            grid=(steps,),
            in_specs=[
                pl.BlockSpec(block, lambda i, own_at, other_at: (own_at[i], 0, 0, 0)),
                pl.BlockSpec(block, lambda i, own_at, other_at: (other_at[i], 0, 0, 0)),
                pl.BlockSpec((k, width), lambda i, own_at, other_at: (0, 0)),
            ],
            out_specs=pl.BlockSpec((1, NZH, SEQ_LEN, width), lambda i, own_at, other_at: (i, 0, 0, 0)),
        ),
        out_shape=jax.ShapeDtypeStruct((steps, NZH, SEQ_LEN, width), F32),
        compiler_params=pltpu.CompilerParams(vmem_limit_bytes=8 * 1024 * 1024),
        cost_estimate=pl.CostEstimate(
            flops=2 * steps * NZH * SEQ_LEN * k * width, bytes_accessed=k * width * 2, transcendentals=0
        ),
    )(own_at, other_at, own, other, basis)


class Inputs:
    def __init__(self, line, basis):
        self.line, self.basis = line, basis

    def rows(self, rows):
        self.g = rows
        self.r = trade(rows, "y", other=True)

    def rows_more(self):
        self.g = self.line.run(lambda r, u: jnp.stack([u, r]), self.r, self.g)
        self.r = trade(self.g, "y")

    def rows_z(self):
        self.g = self.line.run(lambda r, u: jnp.concatenate([u, r], axis=0), self.r, self.g)
        self.r = swap(self.g, "zh")

    def rows_cross(self):
        self.g = self.line.run(lambda r, u: jnp.stack([u, r], axis=1), self.r, self.g)
        self.r = swap(self.g, "core")

    def multiply(self):
        a = near_bit()
        off = lax.axis_index("y") ^ lax.axis_index("x")

        def at(bits, b):
            bits = jnp.stack([off ^ bit for bit in bits])
            return jnp.where(bits == 0, 0, jnp.where(bits == 2, 3, jnp.where(bits == b, 1, 2)))

        def step(r, g, bits):
            return part_sums(at(bits, 4 - a), at(bits, a), g, r, self.basis)

        send = self.line.run(lambda r, g: step(r, g, (a, 2)), self.r, self.g)
        other = self.r
        self.r = trade(send, "x")
        self.here = self.line.run(lambda r, g: step(r, g, (0, 4 - a)), other, self.g)

    def reduce(self):
        send, self.here = self.line.run(lambda r, u: (u[1] + r[1], u[0] + r[0]), self.r, self.here)
        self.r = trade(send, "x", other=True)

    def exchange(self):
        self.here = self.line.run(lambda r, u: u + r, self.r, self.here)
        self.r = swap(self.here, "zl")

    def gather(self):
        flip = lax.axis_index("zl") ^ lax.axis_index("zh")

        def step(r, u):
            total = (u + r).astype(BF)
            return to_gather_order(jnp.stack([pick(total, flip, 0), pick(total, 1 - flip, 0)]))

        self.g = self.line.run(step, self.r, self.here)
        self.r = trade(self.g, "x", other=True)

    def gather_more(self):
        self.g = self.line.run(lambda r, u: jnp.stack([u, r]), self.r, self.g)
        self.r = trade(self.g, "x")

    def all(self):
        straight = near_bit() == 1

        def step(r, g):
            one, three = jnp.where(straight, r[0], g[1]), jnp.where(straight, g[1], r[0])
            return jnp.stack([g[0, 0], g[0, 1], one[0], three[0], one[1], three[1], r[1, 0], r[1, 1]])

        return self.line.run(step, self.r, self.g)


def square_kernel(sizes, *refs):
    x_ref, out_ref = refs[-2], refs[-1]
    s = 0
    for c, n in enumerate(sizes):
        own, other = refs[2 * c], refs[2 * c + 1]
        for i in range(n):
            g = jnp.concatenate([own[i], other[i]], axis=0)
            p = lax.dot_general(g, x_ref[s], (((0,), (0,)), ((), ())), preferred_element_type=F32)
            if s == 0:
                out_ref[...] = p * p
            else:
                out_ref[...] += p * p
            s += 1
    out_ref[...] *= 1.0 / s


def square_sum(chunks, inputs):
    sizes = tuple(own.shape[0] for own, _ in chunks)
    rows = chunks[0][0].shape[2]
    cols = inputs.shape[2]
    tile = rows // 4
    specs = []
    operands = []
    for own, other in chunks:
        for v in (own, other):
            specs.append(pl.BlockSpec((v.shape[0], v.shape[1], tile), lambda i: (0, 0, i)))
            operands.append(v)
    specs.append(pl.BlockSpec(inputs.shape, lambda i: (0, 0, 0)))
    return pl.pallas_call(
        lambda *refs: square_kernel(sizes, *refs),
        grid=(rows // tile,),
        in_specs=specs,
        out_specs=pl.BlockSpec((tile, cols), lambda i: (i, 0)),
        out_shape=jax.ShapeDtypeStruct((rows, cols), F32),
        compiler_params=pltpu.CompilerParams(vmem_limit_bytes=20 * 1024 * 1024),
        cost_estimate=pl.CostEstimate(
            flops=2 * sum(sizes) * SEQ_LEN * rows * cols, bytes_accessed=rows * cols * 4, transcendentals=0
        ),
    )(*operands, inputs)


def body(out_grads, layer_inputs, basis_out, basis_in):
    line = Line()
    one, two, three = (Chunk(line, basis_out, n) for n in (4, 2, 2))
    inputs = Inputs(line, basis_in)
    half = SEQ_LEN // 2

    def by_bit(first, second):
        straight = near_bit() == 1
        return [jnp.where(straight, first, second), jnp.where(straight, second, first)]

    inputs.rows(layer_inputs)
    own = to_send_order(out_grads)
    near = swap(own, "zl")
    first, second = trade(own, "x"), trade(own, "x", other=True)
    one.multiply_own(own)
    inputs.rows_more()
    near = line.put(near)
    first_n, second_n = trade(near, "x"), trade(near, "x", other=True)
    one.multiply(lambda u, v: [near] + by_bit(u, v), first, second)
    inputs.rows_z()
    one.blocks()
    low = trade(line.run(lambda v, u: jnp.stack([u[:half], v[:half]]), second_n, second), "x")
    high = trade(line.run(lambda v, u: jnp.stack([u[half:], v[half:]]), first_n, first), "x", other=True)
    two.multiply(by_bit, first_n, second_n)
    inputs.rows_cross()
    two.blocks()
    inputs.multiply()
    one.reduce()
    three.multiply(lambda v, u: list(jnp.concatenate([u, v], axis=1)), high, low)
    three.blocks()
    one.exchange()
    two.reduce()
    inputs.reduce()
    three.reduce()
    two.exchange()
    one.gather()
    three.exchange()
    inputs.exchange()
    two.gather()
    one.gather_more()
    three.gather()
    two.gather_more()
    inputs.gather()
    three.gather_more()
    one.cross_back()
    inputs.gather_more()
    two.cross_back()
    three.cross_back()
    x_rows = inputs.all()
    return square_sum([(c.own, c.other) for c in (one, two, three)], x_rows)


def solution(mesh):
    fine = Mesh(mesh.devices.reshape(NX, NZL, NY, NZH, NC), ("x", "zl", "y", "zh", "core"))
    out, inn = ("x", "zl"), ("y", "zh", "core")
    return jax.shard_map(
        body,
        mesh=fine,
        in_specs=(P(out, inn), P(inn, out), P(inn, out), P(out, inn)),
        out_specs=P(out, inn),
        check_vma=False,
    )
```
